32 devices in a mesh: plane: 8 (over z, x), strip: 4 (over y, core).
Axes of the slice: x: 2, y: 2, z: 4, core: 2. Of those that a mesh axis runs over, the one named last changes fastest.
Arguments:
- current: float32 [8, 256, 3072], P('plane', 'strip'), may hold values from -60 to 60, as said below
- cond_x: bfloat16 [8, 256, 3072], P('plane', 'strip'), may hold values from 0.5 to 5
- cond_y: bfloat16 [8, 256, 3072], P('plane', 'strip'), may hold values from 0.5 to 5
- tile_class: int32 [8, 16, 24], P('plane', 'strip'), may hold values from 0 to 7
- class_diag: float32 [8], replicated, may hold values from 0.2 to 2
- via_count: int32 [8, 16, 24], P('plane', 'strip'), may hold values from 0 to 3, as said below
Outputs:
- voltage: float32 [8, 256, 3072], P('plane', 'strip')
- residual_ratio: float32 [4, 8], P(None, 'plane')
The draws below stay inside these ranges and needn't reach their ends.
Inputs may be any that keep to these rules, and one draw needn't show every extreme that they name: `current`: load currents; any value in the range. `via_count`: in the rows of one device of each plane exactly 24 tiles have a nonzero count; planes 2k and 2k + 1 have equal counts everywhere.
All inputs are finite; a program needn't handle non-finite values.
Results may differ from the reference program's by a relative error of at most 0.0003.
Values sent between devices are 32-bit elements; how exact they have to be, the bound alone decides.
A program may use at most 64 MiB of HBM per device.

```python
import math
import jax
import jax.numpy as jnp
from jax import lax

ROW_DEV = 64
COLS = 3072
TILE_ROWS = 16
TILE_COLS = 128
CLASSES = 8
SWEEPS = 4
PLANES = 8
ROWS = 256
VIA_TILES = 24


def draw_current(key, part):
    shape = (PLANES, ROWS, COLS)
    rows = jnp.arange(ROWS, dtype=jnp.float32) / max(ROWS - 1, 1)
    ramp = jnp.exp(jnp.log(3.0) * rows)[None, :, None]
    base = jnp.clip(jax.random.normal(key, shape, jnp.float32), -5.0, 5.0)
    return (4.0 * base * ramp).astype(jnp.float32)


def draw_via_count(key, part):
    tile_rows = ROW_DEV // TILE_ROWS
    tile_cols = COLS // TILE_COLS
    blocks = ROWS // ROW_DEV
    pairs = PLANES // 2
    count_all = tile_rows * tile_cols

    def one_block(pair, block):
        inner = jax.random.fold_in(jax.random.fold_in(key, pair), block)
        order = jax.random.permutation(jax.random.fold_in(inner, 1), count_all)
        counts = jax.random.randint(jax.random.fold_in(inner, 2), (count_all,), 1, 4)
        return jnp.where(order < VIA_TILES, counts, 0).reshape(tile_rows, tile_cols)
    grid = jax.vmap(jax.vmap(one_block, (None, 0)), (0, None))(jnp.arange(pairs), jnp.arange(blocks))
    grid = grid.reshape(pairs, blocks * tile_rows, tile_cols)
    return jnp.repeat(grid, 2, axis=0).astype(jnp.int32)


def place_ends(values, stream_key, smallest, high):
    dims = values.shape
    index_at = [jax.random.randint(jax.random.fold_in(stream_key, axis), (), 0, dims[axis]) for axis in range(len(dims))]
    values = values.at[tuple(index_at)].set(smallest)
    longest = dims.index(max(dims))
    index_at[longest] = (index_at[longest] + 1) % dims[longest]
    return values.at[tuple(index_at)].set(high)


def steps_of(stream_key, dims, cuts, smallest, top_value):
    level, own = 1.0, jax.random.fold_in(stream_key, 6)
    for position, shards_of in cuts:
        steps = jnp.exp(jax.random.uniform(jax.random.fold_in(own, position), (shards_of,), jnp.float32, smallest / len(cuts), top_value / len(cuts)))
        level = level * jnp.repeat(steps, dims[position] // shards_of).reshape([-1 if axis == position else 1 for axis in range(len(dims))])
    return level


def setup_inputs(seed: int = 0) -> dict:
    seeds = jax.random.split(jax.random.key(seed), 7)
    return {
        "current": draw_current(jax.random.fold_in(seeds[6], 71), 0),
        "cond_x": jnp.clip(jnp.exp(math.log(5.0) - 2.3025851 * jax.random.uniform(seeds[1], (PLANES, ROWS, COLS), jnp.float32) ** steps_of(seeds[1], (PLANES, ROWS, COLS), ((0, 8), (1, 4)), -0.2, 0.2)), 0.5, 5.0).astype(jnp.bfloat16),
        "cond_y": jnp.clip(jnp.exp(math.log(5.0) - 2.3025851 * jax.random.uniform(seeds[2], (PLANES, ROWS, COLS), jnp.float32) ** steps_of(seeds[2], (PLANES, ROWS, COLS), ((0, 8), (1, 4)), -0.2, 0.2)), 0.5, 5.0).astype(jnp.bfloat16),
        "tile_class": place_ends(jax.random.randint(seeds[3], (PLANES, ROWS // TILE_ROWS, COLS // TILE_COLS), 0, CLASSES), jax.random.fold_in(seeds[3], 1), 0, CLASSES - 1).astype(jnp.int32),
        "class_diag": jnp.clip(jnp.exp(jax.random.uniform(seeds[4], (CLASSES,), jnp.float32, math.log(0.2), math.log(2.0))), 0.2, 2.0),
        "via_count": draw_via_count(jax.random.fold_in(seeds[6], 71), 0),
    }


ground_cond = 0.5
via_cond = 3.0
bound_low = 0.05
bound_high = 2.0

def cheby_coeffs(sweeps):
    theta = (bound_high + bound_low) / 2.0
    delta = (bound_high - bound_low) / 2.0
    sigma = theta / delta
    rho = 1.0 / sigma
    coeffs = []
    for step in range(sweeps - 1):
        rho_new = 1.0 / (2.0 * sigma - rho)
        coeffs.append((rho_new * rho, 2.0 * rho_new / delta))
        rho = rho_new
    return (theta, coeffs)

def expand(tiles):
    return jnp.repeat(jnp.repeat(tiles, TILE_ROWS, axis=1), TILE_COLS, axis=2)

def shift_rows(field):
    return jnp.pad(field, ((0, 0), (1, 0), (0, 0)))[:, :-1, :]

def shift_cols(field):
    return jnp.pad(field, ((0, 0), (0, 0), (1, 0)))[:, :, :-1]

def reference(current, cond_x, cond_y, tile_class, class_diag, via_count):
    horiz = cond_x.astype(jnp.float32)
    vert = cond_y.astype(jnp.float32)
    picked = tile_class[..., None] == jnp.arange(CLASSES, dtype=jnp.int32)
    lookup = lax.optimization_barrier(jnp.sum(jnp.where(picked, class_diag, jnp.float32(0.0)), axis=-1))
    diagl = expand(lookup)
    via_g = via_cond * expand(via_count.astype(jnp.float32))
    horiz_left = shift_cols(horiz)
    vert_up = shift_rows(vert)
    diag_up = shift_rows(diagl)
    diag_left = shift_cols(diagl)
    diag_upleft = shift_cols(diag_up)
    center = ground_cond + horiz + horiz_left + vert + vert_up + diagl + diag_upleft + diag_left + diag_up + via_g
    rows, cols = (current.shape[1], current.shape[2])

    def apply(field):
        padded = jnp.pad(field, ((0, 0), (1, 1), (1, 1)))

        def near(di, dj):
            return padded[:, 1 + di:1 + di + rows, 1 + dj:1 + dj + cols]
        beside = horiz * near(0, 1) + horiz_left * near(0, -1)
        beside = beside + vert * near(1, 0) + vert_up * near(-1, 0)
        beside = beside + diagl * near(1, 1) + diag_upleft * near(-1, -1)
        beside = beside + diag_left * near(1, -1) + diag_up * near(-1, 1)
        partner = field.reshape(PLANES // 2, 2, rows, cols)[:, ::-1].reshape(PLANES, rows, cols)
        return center * field - beside - via_g * partner
    theta, coeffs = cheby_coeffs(SWEEPS)
    source = lax.optimization_barrier(jnp.sum(current * current, axis=(1, 2)))
    voltage = jnp.zeros_like(current)
    residual = current
    direction = residual / (theta * center)
    ratios = []
    for step in range(SWEEPS):
        voltage = voltage + direction
        residual = residual - apply(direction)
        ratios.append(jnp.sqrt(lax.optimization_barrier(jnp.sum(residual * residual, axis=(1, 2))) / source))
        if step < SWEEPS - 1:
            keep, push = coeffs[step]
            direction = keep * direction + push * residual / center
    return (voltage, jnp.stack(ratios))
```

```python
import functools

import jax
import jax.numpy as jnp
from jax import lax
from jax.experimental import pallas as pl
from jax.experimental.pallas import tpu as pltpu
from jax.sharding import PartitionSpec as P

TILE_ROWS = 16
TILE_COLS = 128
SWEEPS = 4
VIA_TILES = 24
CHUNKS = 3
WIDE = 3

ground_cond = 0.5
via_cond = 3.0
bound_low = 0.05
bound_high = 2.0

MESH = pl.DeviceIdType.MESH


def cheby_coeffs(sweeps):
    theta = (bound_high + bound_low) / 2.0
    delta = (bound_high - bound_low) / 2.0
    sigma = theta / delta
    rho = 1.0 / sigma
    coeffs = []
    for step in range(sweeps - 1):
        rho_new = 1.0 / (2.0 * sigma - rho)
        coeffs.append((rho_new * rho, 2.0 * rho_new / delta))
        rho = rho_new
    return (theta, coeffs)


def kernel(
    n_strip,
    cur_hbm, cx_hbm, cy_hbm, cls, cdiag, via,
    volt_hbm, ratio_ref,
    cur, cx, cy, volt, dbuf, gxf, gyf, gdrow, cen, inv, w, res,
    send, recv0, recv1, recv2, recv3, hs, hr, cs, cr, sums, sums_in,
    nxt, idx, pos,
    load_sem, out_sem, ps_sem, pr_sem, hs_sem, hr_sem, cs_sem, cr_sem, ss_sem, sr_sem,
):
    recv = (recv0, recv1, recv2, recv3)
    rows, cols = cur.shape
    tr, tc = rows // TILE_ROWS, cols // TILE_COLS
    tiles = tr * tc
    slots = VIA_TILES // CHUNKS
    theta, coeffs = cheby_coeffs(SWEEPS)
    my_plane = lax.axis_index("plane")
    me = lax.axis_index("strip")
    partner = my_plane + 1 - 2 * (my_plane % 2)
    has_up = me > 0
    has_down = me < n_strip - 1

    loads = [
        pltpu.make_async_copy(cy_hbm, cy, load_sem.at[0]),
        pltpu.make_async_copy(cx_hbm, cx, load_sem.at[1]),
        pltpu.make_async_copy(cur_hbm, cur, load_sem.at[2]),
    ]
    for copy in loads:
        copy.start()

    barrier = pltpu.get_barrier_semaphore()
    pl.semaphore_signal(barrier, inc=1, device_id={"plane": partner}, device_id_type=MESH)
    for off in range(1, n_strip):
        pl.semaphore_signal(
            barrier, inc=1, device_id={"strip": (me + off) % n_strip}, device_id_type=MESH
        )

    lane = lax.broadcasted_iota(jnp.int32, (TILE_ROWS, TILE_COLS), 1)
    row_id = lax.broadcasted_iota(jnp.int32, (TILE_ROWS, TILE_COLS), 0)
    first_lane, last_lane, first_row = lane == 0, lane == TILE_COLS - 1, row_id == 0

    def lanes(c):
        if isinstance(c, int):
            return pl.ds(c * TILE_COLS, TILE_COLS)
        return pl.ds(pl.multiple_of(c * TILE_COLS, TILE_COLS), TILE_COLS)

    for k in range(SWEEPS):
        dbuf[k, 0:8, :] = jnp.zeros((8, cols + TILE_COLS), jnp.float32)
        dbuf[k, rows + 8 : rows + 16, :] = jnp.zeros((8, cols + TILE_COLS), jnp.float32)
        dbuf[k, 8 : rows + 8, cols : cols + TILE_COLS] = jnp.zeros((rows, TILE_COLS), jnp.float32)
    gdrow[...] = jnp.zeros_like(gdrow)
    gyf[0:8, :] = jnp.zeros((8, cols), jnp.float32)

    for r in range(tr):
        def fill(c, _, r=r):
            g = cdiag[cls[r, c]]
            gdrow[r + 1 : r + 2, lanes(c)] = jnp.full((1, TILE_COLS), g, jnp.float32)
            return 0
        lax.fori_loop(0, tc, fill, 0)

    loads[0].wait()
    cs[0] = cy[rows - TILE_ROWS : rows, :].astype(jnp.float32)[TILE_ROWS - 1 : TILE_ROWS, :]
    cs[1] = gdrow[tr : tr + 1, :]
    pl.semaphore_wait(barrier, n_strip)

    cond_copy = pltpu.make_async_remote_copy(
        src_ref=cs, dst_ref=cr, send_sem=cs_sem, recv_sem=cr_sem,
        device_id={"strip": (me + 1) % n_strip}, device_id_type=MESH,
    )

    @pl.when(has_down)
    def _():
        cond_copy.start()

    nxt[tiles] = 0
    for r in reversed(range(tr)):
        def back(i, follow, r=r):
            c = tc - 1 - i
            t = r * tc + c
            here = jnp.where(via[r, c] > 0, t, follow)
            nxt[t] = here
            return here
        follow = lax.fori_loop(0, tc, back, jnp.int32(0) if r == tr - 1 else follow)
    count = jnp.int32(0)
    for r in range(tr):
        def forth(c, count, r=r):
            pos[r * tc + c] = jnp.minimum(count, VIA_TILES - 1)
            return count + jnp.where(via[r, c] > 0, 1, 0)
        count = lax.fori_loop(0, tc, forth, count)

    def chain(s, t):
        here = nxt[t]
        idx[s] = here
        return here + 1
    lax.fori_loop(0, VIA_TILES, chain, jnp.int32(0))

    loads[1].wait()

    def convert(c, _):
        gxf[:, lanes(c)] = cx[:, lanes(c)].astype(jnp.float32)
        gyf[8 : rows + 8, lanes(c)] = cy[:, lanes(c)].astype(jnp.float32)
        return 0
    lax.fori_loop(0, tc, convert, 0)
    loads[2].wait()

    def coupling(r, c):
        g = gdrow[r + 1 : r + 2, lanes(c)]
        up = gdrow[r : r + 1, lanes(c)]
        g = jnp.broadcast_to(g, (TILE_ROWS, TILE_COLS))
        return g, jnp.where(first_row, jnp.broadcast_to(up, (TILE_ROWS, TILE_COLS)), g)

    zero = jnp.zeros((TILE_ROWS, TILE_COLS), jnp.float32)

    def prepare(row_tiles, acc):
        def body(i, carry):
            acc, before = carry[0], list(carry[1:])
            for j in range(WIDE):
                c = i * WIDE + j
                for q, r in enumerate(row_tiles):
                    t = r * tc + c
                    own = pl.ds(r * TILE_ROWS, TILE_ROWS)
                    g, g_up = coupling(r, c)
                    side = gxf[own, lanes(c)] + g + g_up
                    left = pltpu.roll(jnp.where(last_lane, before[q], side), 1, 1)
                    before[q] = side
                    gv = via_cond * via[r, c].astype(jnp.float32)
                    center = (
                        (ground_cond + gv) + side + left
                        + gyf[pl.ds(8 + r * TILE_ROWS, TILE_ROWS), lanes(c)]
                        + gyf[pl.ds(7 + r * TILE_ROWS, TILE_ROWS), lanes(c)]
                    )
                    inverse = 1.0 / center
                    source = cur[own, lanes(c)]
                    d0 = source * inverse * (1.0 / theta)
                    cen[t] = center
                    inv[t] = inverse
                    res[t] = source
                    w[t] = d0
                    dbuf[0, pl.ds(8 + r * TILE_ROWS, TILE_ROWS), lanes(c)] = d0
                    acc = acc + source * source
            return (acc, *before)
        return lax.fori_loop(0, tc // WIDE, body, (acc,) + (zero,) * len(row_tiles))[0]

    acc = prepare(tuple(range(1, tr)), zero)

    @pl.when(has_up)
    def _():
        cond_copy.wait_recv()
        gyf[7:8, :] = cr[0]
        gdrow[0:1, :] = cr[1]

    acc = prepare((0,), acc)
    sums[...] = jnp.zeros_like(sums)
    sums[0:1, :] = jnp.sum(acc, axis=0, keepdims=True)

    def part_copy(k, ch):
        part = pl.ds(ch * slots, slots)
        return pltpu.make_async_remote_copy(
            src_ref=send.at[k, part], dst_ref=recv[k].at[part],
            send_sem=ps_sem.at[k, ch], recv_sem=pr_sem.at[k, ch],
            device_id={"plane": partner}, device_id_type=MESH,
        )

    def halo_copy(k, side):
        to = (me + n_strip - 1) % n_strip if side == 0 else (me + 1) % n_strip
        return pltpu.make_async_remote_copy(
            src_ref=hs.at[k, side], dst_ref=hr.at[k, side],
            send_sem=hs_sem.at[k, side], recv_sem=hr_sem.at[k, side],
            device_id={"strip": to}, device_id_type=MESH,
        )

    def send_halos(k):
        hs[k, 0] = dbuf[k, 8:9, 0:cols]
        hs[k, 1] = dbuf[k, rows + 7 : rows + 8, 0:cols]

        @pl.when(has_up)
        def _():
            halo_copy(k, 0).start()

        @pl.when(has_down)
        def _():
            halo_copy(k, 1).start()

    def take_halos(k):
        @pl.when(has_up)
        def _():
            halo_copy(k, 1).wait_recv()
            dbuf[k, 7:8, 0:cols] = hr[k, 1]

        @pl.when(has_down)
        def _():
            halo_copy(k, 0).wait_recv()
            dbuf[k, rows + 8 : rows + 9, 0:cols] = hr[k, 0]

    for ch in range(CHUNKS):
        def pack(s, _):
            send[0, s] = w[idx[s]]
            return 0
        lax.fori_loop(ch * slots, (ch + 1) * slots, pack, 0)
        part_copy(0, ch).start()
    send_halos(0)

    def stencil(k, row_tiles, acc):
        last = k == SWEEPS - 1

        def body(i, carry):
            acc, before = carry[0], list(carry[1:])
            for q, r in enumerate(row_tiles):
                base = 8 + r * TILE_ROWS

                def load(off, c):
                    return dbuf[k, pl.ds(base + off, TILE_ROWS), lanes(c)]

                ahead = [load(off, i * WIDE) for off in (0, -1, 1)]
                for j in range(WIDE):
                    c = i * WIDE + j
                    t = r * tc + c
                    mid, north, south = ahead
                    ahead = [load(off, c + 1) for off in (0, -1, 1)]
                    g, g_up = coupling(r, c)
                    gx = gxf[pl.ds(r * TILE_ROWS, TILE_ROWS), lanes(c)]
                    gy = gyf[pl.ds(base, TILE_ROWS), lanes(c)]
                    gy_up = gyf[pl.ds(base - 1, TILE_ROWS), lanes(c)]
                    cross = g * south + g_up * north
                    cross_ahead = g * ahead[2] + g_up * ahead[1]
                    side = gx * mid + cross
                    east = pltpu.roll(jnp.where(first_lane, ahead[0], mid), TILE_COLS - 1, 1)
                    east_cross = pltpu.roll(
                        jnp.where(first_lane, cross_ahead, cross), TILE_COLS - 1, 1
                    )
                    west = pltpu.roll(jnp.where(last_lane, before[q], side), 1, 1)
                    before[q] = side
                    beside = (gx * east + east_cross) + west + (gy * south + gy_up * north)
                    left = res[t] - cen[t] * mid + beside
                    res[t] = left
                    if last:
                        plain = jnp.where(via[r, c] > 0, 0.0, 1.0)
                        acc = acc + plain * (left * left)
                    else:
                        keep, push = coeffs[k]
                        w[t] = keep * mid + push * (inv[t] * left)
            return (acc, *before)
        return lax.fori_loop(0, tc // WIDE, body, (acc,) + (zero,) * len(row_tiles))[0]

    def merge(k, row_tiles, acc):
        push = coeffs[k][1]

        def body(i, acc):
            for j in range(WIDE):
                c = i * WIDE + j
                for r in row_tiles:
                    t = r * tc + c
                    gv = via_cond * via[r, c].astype(jnp.float32)
                    term = gv * recv[k][pos[t]]
                    left = res[t] + term
                    res[t] = left
                    acc = acc + left * left
                    dbuf[k + 1, pl.ds(8 + r * TILE_ROWS, TILE_ROWS), lanes(c)] = (
                        w[t] + push * (inv[t] * term)
                    )
            return acc
        return lax.fori_loop(0, tc // WIDE, body, acc)

    edge_tiles = (0, tr - 1)
    inner_tiles = tuple(range(1, tr - 1))

    def via_of(t):
        return via[t // tc, t % tc].astype(jnp.float32)

    out_copy = pltpu.make_async_copy(volt, volt_hbm, out_sem)
    for k in range(SWEEPS):
        acc = stencil(k, inner_tiles, zero)
        take_halos(k)
        acc = stencil(k, edge_tiles, acc)
        if k < SWEEPS - 1:
            push = coeffs[k][1]
            for ch in range(CHUNKS):
                part_copy(k, ch).wait_recv()

                def next_slot(s, _):
                    t = idx[s]
                    term = (via_cond * via_of(t)) * recv[k][s]
                    send[k + 1, s] = w[t] + push * (inv[t] * term)
                    return 0
                lax.fori_loop(ch * slots, (ch + 1) * slots, next_slot, 0)
                part_copy(k + 1, ch).start()
            acc = merge(k, edge_tiles, zero)
            send_halos(k + 1)
            acc = merge(k, inner_tiles, acc)
        else:
            def total(c, _):
                own = pl.ds(8, rows)
                volt[:, lanes(c)] = (
                    dbuf[0, own, lanes(c)] + dbuf[1, own, lanes(c)]
                    + dbuf[2, own, lanes(c)] + dbuf[3, own, lanes(c)]
                )
                return 0
            lax.fori_loop(0, tc, total, 0)
            out_copy.start()
            for ch in range(CHUNKS):
                part_copy(k, ch).wait_recv()

                def last_slot(s, acc):
                    t = idx[s]
                    left = res[t] + (via_cond * via_of(t)) * recv[k][s]
                    return acc + left * left
                acc = lax.fori_loop(ch * slots, (ch + 1) * slots, last_slot, acc)
        sums[k + 1 : k + 2, :] = jnp.sum(acc, axis=0, keepdims=True)

    def sum_copy(off):
        return pltpu.make_async_remote_copy(
            src_ref=sums, dst_ref=sums_in.at[off - 1],
            send_sem=ss_sem.at[off - 1], recv_sem=sr_sem.at[off - 1],
            device_id={"strip": (me + off) % n_strip}, device_id_type=MESH,
        )

    for off in range(1, n_strip):
        sum_copy(off).start()

    @pl.when(has_down)
    def _():
        cond_copy.wait_send()
    for k in range(SWEEPS):
        for ch in range(CHUNKS):
            part_copy(k, ch).wait_send()

        @pl.when(has_up)
        def _():
            halo_copy(k, 0).wait_send()

        @pl.when(has_down)
        def _():
            halo_copy(k, 1).wait_send()

    whole = sums[...]
    for off in range(1, n_strip):
        sum_copy(off).wait_recv()
        whole = whole + sums_in[off - 1]
    whole = jnp.sum(whole, axis=1, keepdims=True)
    ratio_ref[...] = jnp.sqrt(whole[1 : SWEEPS + 1, :] / whole[0:1, :])
    for off in range(1, n_strip):
        sum_copy(off).wait_send()
    out_copy.wait()


def solution(mesh):
    n_strip = mesh.shape["strip"]

    def on_device(current, cond_x, cond_y, tile_class, class_diag, via_count):
        rows, cols = current.shape[1:]
        tr, tc = rows // TILE_ROWS, cols // TILE_COLS
        tiles = tr * tc
        f32 = jnp.float32
        tile = (tiles, TILE_ROWS, TILE_COLS)
        packed = (SWEEPS, VIA_TILES, TILE_ROWS, TILE_COLS)
        dma = pltpu.SemaphoreType.DMA
        voltage, ratios = pl.pallas_call(
            functools.partial(kernel, n_strip),
            out_shape=(
                jax.ShapeDtypeStruct((rows, cols), f32),
                jax.ShapeDtypeStruct((SWEEPS, 1), f32),
            ),
            in_specs=[pl.BlockSpec(memory_space=pl.ANY)] * 3
            + [pl.BlockSpec(memory_space=pltpu.SMEM)] * 3,
            out_specs=(
                pl.BlockSpec(memory_space=pl.ANY),
                pl.BlockSpec(memory_space=pltpu.VMEM),
            ),
            scratch_shapes=[
                pltpu.VMEM((rows, cols), f32),
                pltpu.VMEM((rows, cols), jnp.bfloat16),
                pltpu.VMEM((rows, cols), jnp.bfloat16),
                pltpu.VMEM((rows, cols), f32),
                pltpu.VMEM((SWEEPS, rows + 16, cols + TILE_COLS), f32),
                pltpu.VMEM((rows, cols), f32),
                pltpu.VMEM((rows + 8, cols), f32),
                pltpu.VMEM((8, cols), f32),
                pltpu.VMEM(tile, f32),
                pltpu.VMEM(tile, f32),
                pltpu.VMEM(tile, f32),
                pltpu.VMEM(tile, f32),
                pltpu.VMEM(packed, f32),
                pltpu.VMEM(packed[1:], f32),
                pltpu.VMEM(packed[1:], f32),
                pltpu.VMEM(packed[1:], f32),
                pltpu.VMEM(packed[1:], f32),
                pltpu.VMEM((SWEEPS, 2, 1, cols), f32),
                pltpu.VMEM((SWEEPS, 2, 1, cols), f32),
                pltpu.VMEM((2, 1, cols), f32),
                pltpu.VMEM((2, 1, cols), f32),
                pltpu.VMEM((8, TILE_COLS), f32),
                pltpu.VMEM((n_strip - 1, 8, TILE_COLS), f32),
                pltpu.SMEM((tiles + 1,), jnp.int32),
                pltpu.SMEM((VIA_TILES,), jnp.int32),
                pltpu.SMEM((tiles,), jnp.int32),
                dma((3,)),
                dma,
                dma((SWEEPS, CHUNKS)),
                dma((SWEEPS, CHUNKS)),
                dma((SWEEPS, 2)),
                dma((SWEEPS, 2)),
                dma,
                dma,
                dma((n_strip - 1,)),
                dma((n_strip - 1,)),
            ],
            compiler_params=pltpu.CompilerParams(
                collective_id=0, has_side_effects=True, vmem_limit_bytes=48 * 1024 * 1024
            ),
            name="cheby",
        )(current[0], cond_x[0], cond_y[0], tile_class[0], class_diag, via_count[0])
        return (voltage[None], ratios)

    placed = (
        P("plane", "strip", None),
        P("plane", "strip", None),
        P("plane", "strip", None),
        P("plane", "strip", None),
        P(),
        P("plane", "strip", None),
    )
    return jax.shard_map(
        on_device,
        mesh=mesh,
        in_specs=placed,
        out_specs=(P("plane", "strip", None), P(None, "plane")),
        check_vma=False,
    )
```

```python
import functools

import jax
import jax.numpy as jnp
from jax import lax
from jax.experimental import pallas as pl
from jax.experimental.pallas import tpu as pltpu
from jax.sharding import PartitionSpec as P

TILE_ROWS = 16
TILE_COLS = 128
SWEEPS = 4
VIA_TILES = 24
CHUNKS = 3
WIDE = 3

ground_cond = 0.5
via_cond = 3.0
bound_low = 0.05
bound_high = 2.0

MESH = pl.DeviceIdType.MESH


def cheby_coeffs(sweeps):
    theta = (bound_high + bound_low) / 2.0
    delta = (bound_high - bound_low) / 2.0
    sigma = theta / delta
    rho = 1.0 / sigma
    coeffs = []
    for step in range(sweeps - 1):
        rho_new = 1.0 / (2.0 * sigma - rho)
        coeffs.append((rho_new * rho, 2.0 * rho_new / delta))
        rho = rho_new
    return (theta, coeffs)


def kernel(
    n_strip,
    cur_hbm, cx_hbm, cy_hbm, cls, cdiag, via,
    volt_hbm, ratio_ref,
    cur, cx, cy, volt, dbuf, gxf, gyf, gdrow, cen, inv, w, res,
    send, recv0, recv1, recv2, recv3, hs, hr, cs, cr, sums, sums_in,
    nxt, idx, pos, via_flat, gvs,
    load_sem, out_sem, ps_sem, pr_sem, hs_sem, hr_sem, cs_sem, cr_sem, ss_sem, sr_sem,
):
    recv = (recv0, recv1, recv2, recv3)
    rows, cols = cur.shape
    tr, tc = rows // TILE_ROWS, cols // TILE_COLS
    tiles = tr * tc
    slots = VIA_TILES // CHUNKS
    theta, coeffs = cheby_coeffs(SWEEPS)
    my_plane = lax.axis_index("plane")
    me = lax.axis_index("strip")
    partner = my_plane + 1 - 2 * (my_plane % 2)
    has_up = me > 0
    has_down = me < n_strip - 1

    loads = [
        pltpu.make_async_copy(cy_hbm, cy, load_sem.at[0]),
        pltpu.make_async_copy(cx_hbm, cx, load_sem.at[1]),
        pltpu.make_async_copy(cur_hbm, cur, load_sem.at[2]),
    ]
    for copy in loads:
        copy.start()

    barrier = pltpu.get_barrier_semaphore()
    pl.semaphore_signal(barrier, inc=1, device_id={"plane": partner}, device_id_type=MESH)
    for off in range(1, n_strip):
        pl.semaphore_signal(
            barrier, inc=1, device_id={"strip": (me + off) % n_strip}, device_id_type=MESH
        )

    lane = lax.broadcasted_iota(jnp.int32, (TILE_ROWS, TILE_COLS), 1)
    row_id = lax.broadcasted_iota(jnp.int32, (TILE_ROWS, TILE_COLS), 0)
    first_lane, last_lane, first_row = lane == 0, lane == TILE_COLS - 1, row_id == 0

    def lanes(c):
        if isinstance(c, int):
            return pl.ds(c * TILE_COLS, TILE_COLS)
        return pl.ds(pl.multiple_of(c * TILE_COLS, TILE_COLS), TILE_COLS)

    for k in range(SWEEPS):
        dbuf[k, 0:8, :] = jnp.zeros((8, cols + TILE_COLS), jnp.float32)
        dbuf[k, rows + 8 : rows + 16, :] = jnp.zeros((8, cols + TILE_COLS), jnp.float32)
        dbuf[k, 8 : rows + 8, cols : cols + TILE_COLS] = jnp.zeros((rows, TILE_COLS), jnp.float32)
    gdrow[...] = jnp.zeros_like(gdrow)
    gyf[0:8, :] = jnp.zeros((8, cols), jnp.float32)

    for r in range(tr):
        def fill(c, _, r=r):
            g = cdiag[cls[r, c]]
            gdrow[r + 1 : r + 2, lanes(c)] = jnp.full((1, TILE_COLS), g, jnp.float32)
            return 0
        lax.fori_loop(0, tc, fill, 0)

    nxt[tiles] = 0
    for r in reversed(range(tr)):
        def back(i, follow, r=r):
            c = tc - 1 - i
            t = r * tc + c
            here = jnp.where(via[r, c] > 0, t, follow)
            nxt[t] = here
            via_flat[t] = via[r, c]
            return here
        follow = lax.fori_loop(0, tc, back, jnp.int32(0) if r == tr - 1 else follow)
    count = jnp.int32(0)
    for r in range(tr):
        def forth(c, count, r=r):
            pos[r * tc + c] = jnp.minimum(count, VIA_TILES - 1)
            return count + jnp.where(via[r, c] > 0, 1, 0)
        count = lax.fori_loop(0, tc, forth, count)

    def chain(s, t):
        here = nxt[t]
        idx[s] = here
        gvs[s] = via_cond * via_flat[here].astype(jnp.float32)
        return here + 1
    lax.fori_loop(0, VIA_TILES, chain, jnp.int32(0))

    loads[0].wait()
    cs[0] = cy[rows - TILE_ROWS : rows, :].astype(jnp.float32)[TILE_ROWS - 1 : TILE_ROWS, :]
    cs[1] = gdrow[tr : tr + 1, :]
    loads[1].wait()

    def convert(c, _):
        gxf[:, lanes(c)] = cx[:, lanes(c)].astype(jnp.float32)
        gyf[8 : rows + 8, lanes(c)] = cy[:, lanes(c)].astype(jnp.float32)
        return 0
    lax.fori_loop(0, tc, convert, 0)
    loads[2].wait()
    pl.semaphore_wait(barrier, n_strip)

    cond_copy = pltpu.make_async_remote_copy(
        src_ref=cs, dst_ref=cr, send_sem=cs_sem, recv_sem=cr_sem,
        device_id={"strip": (me + 1) % n_strip}, device_id_type=MESH,
    )

    @pl.when(has_down)
    def _():
        cond_copy.start()

    def coupling(r, c):
        g = gdrow[r + 1 : r + 2, lanes(c)]
        up = gdrow[r : r + 1, lanes(c)]
        g = jnp.broadcast_to(g, (TILE_ROWS, TILE_COLS))
        return g, jnp.where(first_row, jnp.broadcast_to(up, (TILE_ROWS, TILE_COLS)), g)

    zero = jnp.zeros((TILE_ROWS, TILE_COLS), jnp.float32)

    def prepare(row_tiles, acc):
        def body(i, carry):
            acc, before = carry[0], list(carry[1:])
            for j in range(WIDE):
                c = i * WIDE + j
                for q, r in enumerate(row_tiles):
                    t = r * tc + c
                    own = pl.ds(r * TILE_ROWS, TILE_ROWS)
                    g, g_up = coupling(r, c)
                    side = gxf[own, lanes(c)] + g + g_up
                    left = pltpu.roll(jnp.where(last_lane, before[q], side), 1, 1)
                    before[q] = side
                    gv = via_cond * via[r, c].astype(jnp.float32)
                    center = (
                        (ground_cond + gv) + side + left
                        + gyf[pl.ds(8 + r * TILE_ROWS, TILE_ROWS), lanes(c)]
                        + gyf[pl.ds(7 + r * TILE_ROWS, TILE_ROWS), lanes(c)]
                    )
                    inverse = 1.0 / center
                    source = cur[own, lanes(c)]
                    d0 = source * inverse * (1.0 / theta)
                    cen[t] = center
                    inv[t] = inverse
                    res[t] = source
                    w[t] = d0
                    dbuf[0, pl.ds(8 + r * TILE_ROWS, TILE_ROWS), lanes(c)] = d0
                    acc = acc + source * source
            return (acc, *before)
        return lax.fori_loop(0, tc // WIDE, body, (acc,) + (zero,) * len(row_tiles))[0]

    acc = prepare(tuple(range(1, tr)), zero)

    @pl.when(has_up)
    def _():
        cond_copy.wait_recv()
        gyf[7:8, :] = cr[0]
        gdrow[0:1, :] = cr[1]

    acc = prepare((0,), acc)
    sums[...] = jnp.zeros_like(sums)
    sums[0:1, :] = jnp.sum(acc, axis=0, keepdims=True)

    def part_copy(k, ch):
        part = pl.ds(ch * slots, slots)
        return pltpu.make_async_remote_copy(
            src_ref=send.at[k, part], dst_ref=recv[k].at[part],
            send_sem=ps_sem.at[k, ch], recv_sem=pr_sem.at[k, ch],
            device_id={"plane": partner}, device_id_type=MESH,
        )

    def halo_copy(k, side):
        to = (me + n_strip - 1) % n_strip if side == 0 else (me + 1) % n_strip
        return pltpu.make_async_remote_copy(
            src_ref=hs.at[k, side], dst_ref=hr.at[k, side],
            send_sem=hs_sem.at[k, side], recv_sem=hr_sem.at[k, side],
            device_id={"strip": to}, device_id_type=MESH,
        )

    def send_halos(k):
        hs[k, 0] = dbuf[k, 8:9, 0:cols]
        hs[k, 1] = dbuf[k, rows + 7 : rows + 8, 0:cols]

        @pl.when(has_up)
        def _():
            halo_copy(k, 0).start()

        @pl.when(has_down)
        def _():
            halo_copy(k, 1).start()

    def take_halos(k):
        @pl.when(has_up)
        def _():
            halo_copy(k, 1).wait_recv()
            dbuf[k, 7:8, 0:cols] = hr[k, 1]

        @pl.when(has_down)
        def _():
            halo_copy(k, 0).wait_recv()
            dbuf[k, rows + 8 : rows + 9, 0:cols] = hr[k, 0]

    for ch in range(CHUNKS):
        for s in range(ch * slots, (ch + 1) * slots):
            send[0, s] = w[idx[s]]
        part_copy(0, ch).start()
    send_halos(0)

    def stencil(k, row_tiles, acc):
        last = k == SWEEPS - 1

        def body(i, carry):
            acc, before = carry[0], list(carry[1:])
            for q, r in enumerate(row_tiles):
                base = 8 + r * TILE_ROWS

                def load(off, c):
                    return dbuf[k, pl.ds(base + off, TILE_ROWS), lanes(c)]

                ahead = [load(off, i * WIDE) for off in (0, -1, 1)]
                for j in range(WIDE):
                    c = i * WIDE + j
                    t = r * tc + c
                    mid, north, south = ahead
                    ahead = [load(off, c + 1) for off in (0, -1, 1)]
                    g, g_up = coupling(r, c)
                    gx = gxf[pl.ds(r * TILE_ROWS, TILE_ROWS), lanes(c)]
                    gy = gyf[pl.ds(base, TILE_ROWS), lanes(c)]
                    gy_up = gyf[pl.ds(base - 1, TILE_ROWS), lanes(c)]
                    cross = g * south + g_up * north
                    cross_ahead = g * ahead[2] + g_up * ahead[1]
                    side = gx * mid + cross
                    east = pltpu.roll(jnp.where(first_lane, ahead[0], mid), TILE_COLS - 1, 1)
                    east_cross = pltpu.roll(
                        jnp.where(first_lane, cross_ahead, cross), TILE_COLS - 1, 1
                    )
                    west = pltpu.roll(jnp.where(last_lane, before[q], side), 1, 1)
                    before[q] = side
                    beside = (gx * east + east_cross) + west + (gy * south + gy_up * north)
                    left = res[t] - cen[t] * mid + beside
                    res[t] = left
                    if last:
                        plain = jnp.where(via[r, c] > 0, 0.0, 1.0)
                        acc = acc + plain * (left * left)
                    else:
                        keep, push = coeffs[k]
                        w[t] = keep * mid + push * (inv[t] * left)
            return (acc, *before)
        return lax.fori_loop(0, tc // WIDE, body, (acc,) + (zero,) * len(row_tiles))[0]

    def merge(k, row_tiles, acc):
        push = coeffs[k][1]

        def body(i, acc):
            for j in range(WIDE):
                c = i * WIDE + j
                for r in row_tiles:
                    t = r * tc + c
                    gv = via_cond * via[r, c].astype(jnp.float32)
                    term = gv * recv[k][pos[t]]
                    left = res[t] + term
                    res[t] = left
                    acc = acc + left * left
                    dbuf[k + 1, pl.ds(8 + r * TILE_ROWS, TILE_ROWS), lanes(c)] = (
                        w[t] + push * (inv[t] * term)
                    )
            return acc
        return lax.fori_loop(0, tc // WIDE, body, acc)

    edge_tiles = (0, tr - 1)
    inner_tiles = tuple(range(1, tr - 1))

    out_copy = pltpu.make_async_copy(volt, volt_hbm, out_sem)
    for k in range(SWEEPS):
        acc = stencil(k, inner_tiles, zero)
        take_halos(k)
        acc = stencil(k, edge_tiles, acc)
        if k < SWEEPS - 1:
            push = coeffs[k][1]
            for ch in range(CHUNKS):
                part_copy(k, ch).wait_recv()
                for s in range(ch * slots, (ch + 1) * slots):
                    t = idx[s]
                    send[k + 1, s] = w[t] + (push * gvs[s]) * (inv[t] * recv[k][s])
                part_copy(k + 1, ch).start()
            acc = merge(k, edge_tiles, zero)
            send_halos(k + 1)
            acc = merge(k, inner_tiles, acc)
        else:
            def total(c, _):
                own = pl.ds(8, rows)
                volt[:, lanes(c)] = (
                    dbuf[0, own, lanes(c)] + dbuf[1, own, lanes(c)]
                    + dbuf[2, own, lanes(c)] + dbuf[3, own, lanes(c)]
                )
                return 0
            lax.fori_loop(0, tc, total, 0)
            out_copy.start()
            for ch in range(CHUNKS):
                part_copy(k, ch).wait_recv()
                for s in range(ch * slots, (ch + 1) * slots):
                    left = res[idx[s]] + gvs[s] * recv[k][s]
                    acc = acc + left * left
        sums[k + 1 : k + 2, :] = jnp.sum(acc, axis=0, keepdims=True)

    def sum_copy(off):
        return pltpu.make_async_remote_copy(
            src_ref=sums, dst_ref=sums_in.at[off - 1],
            send_sem=ss_sem.at[off - 1], recv_sem=sr_sem.at[off - 1],
            device_id={"strip": (me + off) % n_strip}, device_id_type=MESH,
        )

    for off in range(1, n_strip):
        sum_copy(off).start()

    @pl.when(has_down)
    def _():
        cond_copy.wait_send()
    for k in range(SWEEPS):
        for ch in range(CHUNKS):
            part_copy(k, ch).wait_send()

        @pl.when(has_up)
        def _():
            halo_copy(k, 0).wait_send()

        @pl.when(has_down)
        def _():
            halo_copy(k, 1).wait_send()

    whole = sums[...]
    for off in range(1, n_strip):
        sum_copy(off).wait_recv()
        whole = whole + sums_in[off - 1]
    whole = jnp.sum(whole, axis=1, keepdims=True)
    at = lax.broadcasted_iota(jnp.int32, (1, SWEEPS), 1)
    ratios = jnp.zeros((1, SWEEPS), jnp.float32)
    for k in range(SWEEPS):
        ratios = jnp.where(at == k, whole[k + 1 : k + 2, :] / whole[0:1, :], ratios)
    ratio_ref[...] = jnp.sqrt(ratios)
    for off in range(1, n_strip):
        sum_copy(off).wait_send()
    out_copy.wait()


def solution(mesh):
    n_strip = mesh.shape["strip"]

    def on_device(current, cond_x, cond_y, tile_class, class_diag, via_count):
        rows, cols = current.shape[1:]
        tr, tc = rows // TILE_ROWS, cols // TILE_COLS
        tiles = tr * tc
        f32 = jnp.float32
        tile = (tiles, TILE_ROWS, TILE_COLS)
        packed = (SWEEPS, VIA_TILES, TILE_ROWS, TILE_COLS)
        dma = pltpu.SemaphoreType.DMA
        voltage, ratios = pl.pallas_call(
            functools.partial(kernel, n_strip),
            out_shape=(
                jax.ShapeDtypeStruct((rows, cols), f32),
                jax.ShapeDtypeStruct((1, SWEEPS), f32),
            ),
            in_specs=[pl.BlockSpec(memory_space=pltpu.HBM)] * 3
            + [pl.BlockSpec(memory_space=pltpu.SMEM)] * 3,
            out_specs=(
                pl.BlockSpec(memory_space=pl.ANY),
                pl.BlockSpec(memory_space=pltpu.VMEM),
            ),
            scratch_shapes=[
                pltpu.VMEM((rows, cols), f32),
                pltpu.VMEM((rows, cols), jnp.bfloat16),
                pltpu.VMEM((rows, cols), jnp.bfloat16),
                pltpu.VMEM((rows, cols), f32),
                pltpu.VMEM((SWEEPS, rows + 16, cols + TILE_COLS), f32),
                pltpu.VMEM((rows, cols), f32),
                pltpu.VMEM((rows + 8, cols), f32),
                pltpu.VMEM((8, cols), f32),
                pltpu.VMEM(tile, f32),
                pltpu.VMEM(tile, f32),
                pltpu.VMEM(tile, f32),
                pltpu.VMEM(tile, f32),
                pltpu.VMEM(packed, f32),
                pltpu.VMEM(packed[1:], f32),
                pltpu.VMEM(packed[1:], f32),
                pltpu.VMEM(packed[1:], f32),
                pltpu.VMEM(packed[1:], f32),
                pltpu.VMEM((SWEEPS, 2, 1, cols), f32),
                pltpu.VMEM((SWEEPS, 2, 1, cols), f32),
                pltpu.VMEM((2, 1, cols), f32),
                pltpu.VMEM((2, 1, cols), f32),
                pltpu.VMEM((8, TILE_COLS), f32),
                pltpu.VMEM((n_strip - 1, 8, TILE_COLS), f32),
                pltpu.SMEM((tiles + 1,), jnp.int32),
                pltpu.SMEM((VIA_TILES,), jnp.int32),
                pltpu.SMEM((tiles,), jnp.int32),
                pltpu.SMEM((tiles,), jnp.int32),
                pltpu.SMEM((VIA_TILES,), f32),
                dma((3,)),
                dma,
                dma((SWEEPS, CHUNKS)),
                dma((SWEEPS, CHUNKS)),
                dma((SWEEPS, 2)),
                dma((SWEEPS, 2)),
                dma,
                dma,
                dma((n_strip - 1,)),
                dma((n_strip - 1,)),
            ],
            compiler_params=pltpu.CompilerParams(
                collective_id=0, has_side_effects=True, vmem_limit_bytes=62 * 1024 * 1024
            ),
            name="cheby",
        )(current[0], cond_x[0], cond_y[0], tile_class[0], class_diag, via_count[0])
        return (voltage[None], ratios.T)

    placed = (
        P("plane", "strip", None),
        P("plane", "strip", None),
        P("plane", "strip", None),
        P("plane", "strip", None),
        P(),
        P("plane", "strip", None),
    )
    return jax.shard_map(
        on_device,
        mesh=mesh,
        in_specs=placed,
        out_specs=(P("plane", "strip", None), P(None, "plane")),
        check_vma=False,
    )
```

```python
import functools

import jax
import jax.numpy as jnp
from jax import lax
from jax.experimental import pallas as pl
from jax.experimental.pallas import tpu as pltpu
from jax.sharding import PartitionSpec as P

TILE_ROWS = 16
TILE_COLS = 128
SWEEPS = 4
VIA_TILES = 24
CHUNKS = 3
WIDE = 3

ground_cond = 0.5
via_cond = 3.0
bound_low = 0.05
bound_high = 2.0

MESH = pl.DeviceIdType.MESH


def cheby_coeffs(sweeps):
    theta = (bound_high + bound_low) / 2.0
    delta = (bound_high - bound_low) / 2.0
    sigma = theta / delta
    rho = 1.0 / sigma
    coeffs = []
    for step in range(sweeps - 1):
        rho_new = 1.0 / (2.0 * sigma - rho)
        coeffs.append((rho_new * rho, 2.0 * rho_new / delta))
        rho = rho_new
    return (theta, coeffs)


def kernel(
    n_strip,
    cur_hbm, cx_hbm, cy_hbm, cls, cdiag, via,
    volt_hbm, ratio_ref,
    cur, cx, cy, volt, dbuf, gxf, gyf, gdrow, cen, inv, w, res,
    send, recv0, recv1, recv2, recv3, hs, hr, cs, cr, sums, sums_in,
    nxt, idx, pos, via_flat, gvs,
    load_sem, out_sem, ps_sem, pr_sem, hs_sem, hr_sem, cs_sem, cr_sem, ss_sem, sr_sem,
):
    recv = (recv0, recv1, recv2, recv3)
    rows, cols = cur.shape
    tr, tc = rows // TILE_ROWS, cols // TILE_COLS
    tiles = tr * tc
    slots = VIA_TILES // CHUNKS
    theta, coeffs = cheby_coeffs(SWEEPS)
    my_plane = lax.axis_index("plane")
    me = lax.axis_index("strip")
    partner = my_plane + 1 - 2 * (my_plane % 2)
    has_up = me > 0
    has_down = me < n_strip - 1

    loads = [
        pltpu.make_async_copy(cy_hbm, cy, load_sem.at[0]),
        pltpu.make_async_copy(cx_hbm, cx, load_sem.at[1]),
        pltpu.make_async_copy(cur_hbm, cur, load_sem.at[2]),
    ]
    for copy in loads:
        copy.start()

    barrier = pltpu.get_barrier_semaphore()
    pl.semaphore_signal(barrier, inc=1, device_id={"plane": partner}, device_id_type=MESH)
    for off in range(1, n_strip):
        pl.semaphore_signal(
            barrier, inc=1, device_id={"strip": (me + off) % n_strip}, device_id_type=MESH
        )

    lane = lax.broadcasted_iota(jnp.int32, (TILE_ROWS, TILE_COLS), 1)
    row_id = lax.broadcasted_iota(jnp.int32, (TILE_ROWS, TILE_COLS), 0)
    first_lane, last_lane, first_row = lane == 0, lane == TILE_COLS - 1, row_id == 0

    def lanes(c):
        if isinstance(c, int):
            return pl.ds(c * TILE_COLS, TILE_COLS)
        return pl.ds(pl.multiple_of(c * TILE_COLS, TILE_COLS), TILE_COLS)

    gdrow[...] = jnp.zeros_like(gdrow)
    gyf[0:8, :] = jnp.zeros((8, cols), jnp.float32)

    for r in range(tr):
        def fill(c, _, r=r):
            g = cdiag[cls[r, c]]
            gdrow[r + 1 : r + 2, lanes(c)] = jnp.full((1, TILE_COLS), g, jnp.float32)
            return 0
        lax.fori_loop(0, tc, fill, 0)

    loads[0].wait()
    cs[0] = cy[rows - TILE_ROWS : rows, :].astype(jnp.float32)[TILE_ROWS - 1 : TILE_ROWS, :]
    cs[1] = gdrow[tr : tr + 1, :]
    pl.semaphore_wait(barrier, n_strip)

    cond_copy = pltpu.make_async_remote_copy(
        src_ref=cs, dst_ref=cr, send_sem=cs_sem, recv_sem=cr_sem,
        device_id={"strip": (me + 1) % n_strip}, device_id_type=MESH,
    )

    @pl.when(has_down)
    def _():
        cond_copy.start()

    nxt[tiles] = 0
    for r in reversed(range(tr)):
        def back(i, follow, r=r):
            c = tc - 1 - i
            t = r * tc + c
            here = jnp.where(via[r, c] > 0, t, follow)
            nxt[t] = here
            via_flat[t] = via[r, c]
            return here
        follow = lax.fori_loop(0, tc, back, jnp.int32(0) if r == tr - 1 else follow)
    def chain(s, t):
        here = nxt[t]
        idx[s] = here
        gvs[s] = via_cond * via_flat[here].astype(jnp.float32)
        return here + 1
    lax.fori_loop(0, VIA_TILES, chain, jnp.int32(0))

    loads[1].wait()

    def convert(c, _):
        gxf[:, lanes(c)] = cx[:, lanes(c)].astype(jnp.float32)
        gyf[8 : rows + 8, lanes(c)] = cy[:, lanes(c)].astype(jnp.float32)
        return 0
    lax.fori_loop(0, tc, convert, 0)
    loads[2].wait()
    def coupling(r, c):
        g = gdrow[r + 1 : r + 2, lanes(c)]
        up = gdrow[r : r + 1, lanes(c)]
        g = jnp.broadcast_to(g, (TILE_ROWS, TILE_COLS))
        return g, jnp.where(first_row, jnp.broadcast_to(up, (TILE_ROWS, TILE_COLS)), g)

    zero = jnp.zeros((TILE_ROWS, TILE_COLS), jnp.float32)

    def prepare(row_tiles, acc):
        def body(i, carry):
            acc, before = carry[0], list(carry[1:])
            for j in range(WIDE):
                c = i * WIDE + j
                for q, r in enumerate(row_tiles):
                    t = r * tc + c
                    own = pl.ds(r * TILE_ROWS, TILE_ROWS)
                    g, g_up = coupling(r, c)
                    side = gxf[own, lanes(c)] + g + g_up
                    left = pltpu.roll(jnp.where(last_lane, before[q], side), 1, 1)
                    before[q] = side
                    gv = via_cond * via[r, c].astype(jnp.float32)
                    center = (
                        (ground_cond + gv) + side + left
                        + gyf[pl.ds(8 + r * TILE_ROWS, TILE_ROWS), lanes(c)]
                        + gyf[pl.ds(7 + r * TILE_ROWS, TILE_ROWS), lanes(c)]
                    )
                    inverse = 1.0 / center
                    source = cur[own, lanes(c)]
                    d0 = source * inverse * (1.0 / theta)
                    cen[t] = center
                    inv[t] = inverse
                    res[t] = source
                    w[t] = d0
                    dbuf[0, pl.ds(8 + r * TILE_ROWS, TILE_ROWS), lanes(c)] = d0
                    acc = acc + source * source
            return (acc, *before)
        return lax.fori_loop(0, tc // WIDE, body, (acc,) + (zero,) * len(row_tiles))[0]

    acc = prepare(tuple(range(1, tr)), zero)

    @pl.when(has_up)
    def _():
        cond_copy.wait_recv()
        gyf[7:8, :] = cr[0]
        gdrow[0:1, :] = cr[1]

    acc = prepare((0,), acc)
    sums[...] = jnp.zeros_like(sums)
    sums[0:1, :] = jnp.sum(acc, axis=0, keepdims=True)

    def part_copy(k, ch):
        part = pl.ds(ch * slots, slots)
        return pltpu.make_async_remote_copy(
            src_ref=send.at[k, part], dst_ref=recv[k].at[part],
            send_sem=ps_sem.at[k, ch], recv_sem=pr_sem.at[k, ch],
            device_id={"plane": partner}, device_id_type=MESH,
        )

    def halo_copy(k, side):
        to = (me + n_strip - 1) % n_strip if side == 0 else (me + 1) % n_strip
        return pltpu.make_async_remote_copy(
            src_ref=hs.at[k, side], dst_ref=hr.at[k, side],
            send_sem=hs_sem.at[k, side], recv_sem=hr_sem.at[k, side],
            device_id={"strip": to}, device_id_type=MESH,
        )

    def send_halos(k):
        hs[k, 0] = dbuf[k, 8:9, 0:cols]
        hs[k, 1] = dbuf[k, rows + 7 : rows + 8, 0:cols]

        @pl.when(has_up)
        def _():
            halo_copy(k, 0).start()

        @pl.when(has_down)
        def _():
            halo_copy(k, 1).start()

    def take_halos(k):
        @pl.when(has_up)
        def _():
            halo_copy(k, 1).wait_recv()
            dbuf[k, 7:8, 0:cols] = hr[k, 1]

        @pl.when(has_down)
        def _():
            halo_copy(k, 0).wait_recv()
            dbuf[k, rows + 8 : rows + 9, 0:cols] = hr[k, 0]

    for ch in range(CHUNKS):
        for s in range(ch * slots, (ch + 1) * slots):
            send[0, s] = w[idx[s]]
        part_copy(0, ch).start()
    send_halos(0)

    count = jnp.int32(0)
    for r in range(tr):
        def forth(c, count, r=r):
            pos[r * tc + c] = jnp.minimum(count, VIA_TILES - 1)
            return count + jnp.where(via[r, c] > 0, 1, 0)
        count = lax.fori_loop(0, tc, forth, count)


    for k in range(SWEEPS):
        dbuf[k, 0:8, :] = jnp.zeros((8, cols + TILE_COLS), jnp.float32)
        dbuf[k, rows + 8 : rows + 16, :] = jnp.zeros((8, cols + TILE_COLS), jnp.float32)
        dbuf[k, 8 : rows + 8, cols : cols + TILE_COLS] = jnp.zeros((rows, TILE_COLS), jnp.float32)

    def stencil(k, row_tiles, acc):
        last = k == SWEEPS - 1

        def body(i, carry):
            acc, before = carry[0], list(carry[1:])
            for q, r in enumerate(row_tiles):
                base = 8 + r * TILE_ROWS

                def load(off, c):
                    return dbuf[k, pl.ds(base + off, TILE_ROWS), lanes(c)]

                ahead = [load(off, i * WIDE) for off in (0, -1, 1)]
                for j in range(WIDE):
                    c = i * WIDE + j
                    t = r * tc + c
                    mid, north, south = ahead
                    ahead = [load(off, c + 1) for off in (0, -1, 1)]
                    g, g_up = coupling(r, c)
                    gx = gxf[pl.ds(r * TILE_ROWS, TILE_ROWS), lanes(c)]
                    gy = gyf[pl.ds(base, TILE_ROWS), lanes(c)]
                    gy_up = gyf[pl.ds(base - 1, TILE_ROWS), lanes(c)]
                    cross = g * south + g_up * north
                    cross_ahead = g * ahead[2] + g_up * ahead[1]
                    side = gx * mid + cross
                    east = pltpu.roll(jnp.where(first_lane, ahead[0], mid), TILE_COLS - 1, 1)
                    east_cross = pltpu.roll(
                        jnp.where(first_lane, cross_ahead, cross), TILE_COLS - 1, 1
                    )
                    west = pltpu.roll(jnp.where(last_lane, before[q], side), 1, 1)
                    before[q] = side
                    beside = (gx * east + east_cross) + west + (gy * south + gy_up * north)
                    left = res[t] - cen[t] * mid + beside
                    res[t] = left
                    if last:
                        plain = jnp.where(via[r, c] > 0, 0.0, 1.0)
                        acc = acc + plain * (left * left)
                    else:
                        keep, push = coeffs[k]
                        w[t] = keep * mid + push * (inv[t] * left)
            return (acc, *before)
        return lax.fori_loop(0, tc // WIDE, body, (acc,) + (zero,) * len(row_tiles))[0]

    def merge(k, row_tiles, acc):
        push = coeffs[k][1]

        def body(i, acc):
            for j in range(WIDE):
                c = i * WIDE + j
                for r in row_tiles:
                    t = r * tc + c
                    gv = via_cond * via[r, c].astype(jnp.float32)
                    term = gv * recv[k][pos[t]]
                    left = res[t] + term
                    res[t] = left
                    acc = acc + left * left
                    dbuf[k + 1, pl.ds(8 + r * TILE_ROWS, TILE_ROWS), lanes(c)] = (
                        w[t] + push * (inv[t] * term)
                    )
            return acc
        return lax.fori_loop(0, tc // WIDE, body, acc)

    edge_tiles = (0, tr - 1)
    inner_tiles = tuple(range(1, tr - 1))

    out_copy = pltpu.make_async_copy(volt, volt_hbm, out_sem)
    for k in range(SWEEPS):
        acc = stencil(k, inner_tiles, zero)
        take_halos(k)
        acc = stencil(k, edge_tiles, acc)
        if k < SWEEPS - 1:
            push = coeffs[k][1]
            for ch in range(CHUNKS):
                part_copy(k, ch).wait_recv()
                for s in range(ch * slots, (ch + 1) * slots):
                    t = idx[s]
                    send[k + 1, s] = w[t] + (push * gvs[s]) * (inv[t] * recv[k][s])
                part_copy(k + 1, ch).start()
            acc = merge(k, edge_tiles, zero)
            send_halos(k + 1)
            acc = merge(k, inner_tiles, acc)
        else:
            def total(c, _):
                own = pl.ds(8, rows)
                volt[:, lanes(c)] = (
                    dbuf[0, own, lanes(c)] + dbuf[1, own, lanes(c)]
                    + dbuf[2, own, lanes(c)] + dbuf[3, own, lanes(c)]
                )
                return 0
            lax.fori_loop(0, tc, total, 0)
            out_copy.start()
            for ch in range(CHUNKS):
                part_copy(k, ch).wait_recv()
                for s in range(ch * slots, (ch + 1) * slots):
                    left = res[idx[s]] + gvs[s] * recv[k][s]
                    acc = acc + left * left
        sums[k + 1 : k + 2, :] = jnp.sum(acc, axis=0, keepdims=True)

    def sum_copy(off):
        return pltpu.make_async_remote_copy(
            src_ref=sums, dst_ref=sums_in.at[off - 1],
            send_sem=ss_sem.at[off - 1], recv_sem=sr_sem.at[off - 1],
            device_id={"strip": (me + off) % n_strip}, device_id_type=MESH,
        )

    for off in range(1, n_strip):
        sum_copy(off).start()

    @pl.when(has_down)
    def _():
        cond_copy.wait_send()
    for k in range(SWEEPS):
        for ch in range(CHUNKS):
            part_copy(k, ch).wait_send()

        @pl.when(has_up)
        def _():
            halo_copy(k, 0).wait_send()

        @pl.when(has_down)
        def _():
            halo_copy(k, 1).wait_send()

    whole = sums[...]
    for off in range(1, n_strip):
        sum_copy(off).wait_recv()
        whole = whole + sums_in[off - 1]
    whole = jnp.sum(whole, axis=1, keepdims=True)
    at = lax.broadcasted_iota(jnp.int32, (1, SWEEPS), 1)
    ratios = jnp.zeros((1, SWEEPS), jnp.float32)
    for k in range(SWEEPS):
        ratios = jnp.where(at == k, whole[k + 1 : k + 2, :] / whole[0:1, :], ratios)
    ratio_ref[...] = jnp.sqrt(ratios)
    for off in range(1, n_strip):
        sum_copy(off).wait_send()
    out_copy.wait()


def solution(mesh):
    n_strip = mesh.shape["strip"]

    def on_device(current, cond_x, cond_y, tile_class, class_diag, via_count):
        rows, cols = current.shape[1:]
        tr, tc = rows // TILE_ROWS, cols // TILE_COLS
        tiles = tr * tc
        f32 = jnp.float32
        tile = (tiles, TILE_ROWS, TILE_COLS)
        packed = (SWEEPS, VIA_TILES, TILE_ROWS, TILE_COLS)
        dma = pltpu.SemaphoreType.DMA
        voltage, ratios = pl.pallas_call(
            functools.partial(kernel, n_strip),
            out_shape=(
                jax.ShapeDtypeStruct((rows, cols), f32),
                jax.ShapeDtypeStruct((1, SWEEPS), f32),
            ),
            in_specs=[pl.BlockSpec(memory_space=pltpu.HBM)] * 3
            + [pl.BlockSpec(memory_space=pltpu.SMEM)] * 3,
            out_specs=(
                pl.BlockSpec(memory_space=pl.ANY),
                pl.BlockSpec(memory_space=pltpu.VMEM),
            ),
            scratch_shapes=[
                pltpu.VMEM((rows, cols), f32),
                pltpu.VMEM((rows, cols), jnp.bfloat16),
                pltpu.VMEM((rows, cols), jnp.bfloat16),
                pltpu.VMEM((rows, cols), f32),
                pltpu.VMEM((SWEEPS, rows + 16, cols + TILE_COLS), f32),
                pltpu.VMEM((rows, cols), f32),
                pltpu.VMEM((rows + 8, cols), f32),
                pltpu.VMEM((8, cols), f32),
                pltpu.VMEM(tile, f32),
                pltpu.VMEM(tile, f32),
                pltpu.VMEM(tile, f32),
                pltpu.VMEM(tile, f32),
                pltpu.VMEM(packed, f32),
                pltpu.VMEM(packed[1:], f32),
                pltpu.VMEM(packed[1:], f32),
                pltpu.VMEM(packed[1:], f32),
                pltpu.VMEM(packed[1:], f32),
                pltpu.VMEM((SWEEPS, 2, 1, cols), f32),
                pltpu.VMEM((SWEEPS, 2, 1, cols), f32),
                pltpu.VMEM((2, 1, cols), f32),
                pltpu.VMEM((2, 1, cols), f32),
                pltpu.VMEM((8, TILE_COLS), f32),
                pltpu.VMEM((n_strip - 1, 8, TILE_COLS), f32),
                pltpu.SMEM((tiles + 1,), jnp.int32),
                pltpu.SMEM((VIA_TILES,), jnp.int32),
                pltpu.SMEM((tiles,), jnp.int32),
                pltpu.SMEM((tiles,), jnp.int32),
                pltpu.SMEM((VIA_TILES,), f32),
                dma((3,)),
                dma,
                dma((SWEEPS, CHUNKS)),
                dma((SWEEPS, CHUNKS)),
                dma((SWEEPS, 2)),
                dma((SWEEPS, 2)),
                dma,
                dma,
                dma((n_strip - 1,)),
                dma((n_strip - 1,)),
            ],
            compiler_params=pltpu.CompilerParams(
                collective_id=0, has_side_effects=True, vmem_limit_bytes=56 * 1024 * 1024
            ),
            name="cheby",
        )(current[0], cond_x[0], cond_y[0], tile_class[0], class_diag, via_count[0])
        return (voltage[None], ratios.T)

    placed = (
        P("plane", "strip", None),
        P("plane", "strip", None),
        P("plane", "strip", None),
        P("plane", "strip", None),
        P(),
        P("plane", "strip", None),
    )
    return jax.shard_map(
        on_device,
        mesh=mesh,
        in_specs=placed,
        out_specs=(P("plane", "strip", None), P(None, "plane")),
        check_vma=False,
    )
```
